32 devices in a mesh: grp: 2 (over y), aa: 4 (over x, core), ba: 4 (over z).
Axes of the slice: x: 2, y: 2, z: 4, core: 2. Of those that a mesh axis runs over, the one named last changes fastest.
Arguments:
- gate_first: bfloat16 [2048, 8192], P(('grp', 'ba'), 'aa'), parts along dimension 0, may hold values from -6 to 6
- up_first: bfloat16 [2048, 8192], P(('grp', 'ba'), 'aa'), parts along dimension 0, may hold values from -6 to 6
- down_first: bfloat16 [8192, 2048], P('aa', ('grp', 'ba')), parts along dimension 1, may hold values from -6 to 6
- gate_second: bfloat16 [57344, 8192], P(('grp', 'ba'), 'aa'), parts along dimension 0, may hold values from -0.0625 to 0.0625
- up_second: bfloat16 [57344, 8192], P(('grp', 'ba'), 'aa'), parts along dimension 0, may hold values from -0.0625 to 0.0625
- down_second: bfloat16 [8192, 57344], P('aa', ('grp', 'ba')), parts along dimension 1, may hold values from -0.0625 to 0.0625
- perm: int32 [16384], P('grp'), parts along dimension 0, may hold values from 0 to 8191, each once
Outputs:
- cost: float32 [2048, 28672], P(('grp', 'aa'), 'ba'), parts along dimension 0
The draws below stay inside these ranges and needn't reach their ends.
There are 2 independent parts, one for each index of `grp`. The reference program is written for one: setup_inputs(seed, part) draws one part's arguments, and reference() takes and returns one part's arrays. A program takes and returns all parts, laid end to end along the dimension named above; each array names one. Nothing has to cross between parts.
All inputs are finite; a program needn't handle non-finite values.
Results may differ from the reference program's by a relative error of at most 0.0003.
Values may be sent and summed in bfloat16 or wider, within the bound.
A program may use at most 320 MiB of HBM per device.

```python
import jax
import jax.numpy as jnp

D = 8192
FF = 28672
PANEL = 1024


def level_of(stream_key, shape, cuts, low, high):
    loudness = 1.0
    for axis_at, parts in cuts:
        steps = jax.random.uniform(jax.random.fold_in(jax.random.fold_in(stream_key, 6), axis_at), (parts,), jnp.float32, low / len(cuts), high / len(cuts))
        loudness = loudness * jnp.repeat(jnp.exp(steps), shape[axis_at] // parts).reshape((-1,) + (1,) * (len(shape) - 1 - axis_at))
    return loudness


def scatter_about(key, shape, deviation, reach, shards=(), held_as=jnp.bfloat16):
    drawn = jax.random.normal(key, shape, jnp.float32) * deviation
    if len(shards) > 0:
        drawn = level_of(key, shape, shards, -0.22, 0.18) * drawn
    return jnp.clip(drawn, min=-reach, max=reach).astype(held_as)


def setup_inputs(seed: int = 0, part: int = 0) -> dict:
    splits = jax.random.split(jax.random.key(seed), 8)
    part_keys = jax.random.split(jax.random.fold_in(splits[7], part), 8)
    return {
        "gate_first": scatter_about(part_keys[0], (PANEL, D), 1.0, 6.0, ((0, 4), (1, 4))),
        "up_first": scatter_about(part_keys[1], (PANEL, D), 1.0, 6.0, ((0, 4), (1, 4))),
        "down_first": scatter_about(part_keys[2], (D, PANEL), 1.0, 6.0, ((0, 4), (1, 4))),
        "gate_second": scatter_about(part_keys[3], (FF, D), D ** -0.5, 0.0625, ((0, 4), (1, 4))),
        "up_second": scatter_about(part_keys[4], (FF, D), D ** -0.5, 0.0625, ((0, 4), (1, 4))),
        "down_second": scatter_about(part_keys[5], (D, FF), D ** -0.5, 0.0625, ((0, 4), (1, 4))),
        "perm": jax.random.permutation(part_keys[6], D).astype(jnp.int32),
    }


def reference(gate_first, up_first, down_first, gate_second, up_second, down_second, perm):
    count_d = perm.shape[0]
    inverse = jnp.zeros((count_d,), jnp.int32).at[perm].set(jnp.arange(count_d, dtype=jnp.int32))
    gate_moved = jnp.take(gate_first, inverse, axis=1)
    up_moved = jnp.take(up_first, inverse, axis=1)
    down_moved = jnp.take(down_first, inverse, axis=0)
    summed = jnp.dot(gate_moved, gate_second.T, preferred_element_type=jnp.float32)
    summed = summed + jnp.dot(up_moved, up_second.T, preferred_element_type=jnp.float32)
    summed = summed + jnp.dot(down_moved.T, down_second, preferred_element_type=jnp.float32)
    return summed
```

```python
import functools

import jax
import jax.numpy as jnp
from jax import lax
from jax.experimental import pallas as pl
from jax.experimental.pallas import tpu as pltpu
from jax.sharding import PartitionSpec as P

MESH = pl.DeviceIdType.MESH
NT_DIMS = (((1,), (1,)), ((), ()))


def kernel(
    stages, blocks, rows, tile, e_tile,
    first_ref, perm_ref, gate_ref, up_ref, down_ref,
    own_ref, far_ref,
    raw, panel, part, near, w_gate, w_up, w_down, onehot,
    w_sem, raw_here, raw_recv, raw_send, z_recv, z_send, near_recv, near_send, far_recv, far_send, own_sem, credit,
):
    columns = first_ref.shape[2]
    units = gate_ref.shape[0]
    half = units // 2
    group = blocks // 4
    a = lax.axis_index("aa")
    b = lax.axis_index("ba")
    core = a + 1 - 2 * (a % 2)
    chip = (a + 2) % 4
    diag = (core + 2) % 4
    has_left, has_right = b > 0, b < blocks - 1
    left, right = jnp.maximum(b - 1, 0), jnp.minimum(b + 1, blocks - 1)

    tiles = units // tile
    split = (tiles + 1) // 2
    halves = ((0, split), (split, tiles))

    def lanes(hh):
        return pl.ds(halves[hh][0] * tile, (halves[hh][1] - halves[hh][0]) * tile)

    def w_copies(t, slot):
        where = pl.ds(t * tile, tile)
        return (
            pltpu.make_async_copy(gate_ref.at[where, :], w_gate.at[slot], w_sem.at[slot, 0]),
            pltpu.make_async_copy(up_ref.at[where, :], w_up.at[slot], w_sem.at[slot, 1]),
            pltpu.make_async_copy(down_ref.at[:, where], w_down.at[slot], w_sem.at[slot, 2]),
        )

    def remote(src, dst, send, recv, **to):
        return pltpu.make_async_remote_copy(
            src_ref=src, dst_ref=dst, send_sem=send, recv_sem=recv, device_id=to, device_id_type=MESH
        )

    def mine(j):
        return first_ref.at[:, pl.ds(j * rows, rows), :]

    def raw_local(j):
        return pltpu.make_async_copy(mine(j), raw.at[j, a], raw_here.at[j])

    def raw_to_chip(j):
        return remote(mine(j), raw.at[j, a], raw_send.at[j, 0], raw_recv.at[j, 0], aa=chip)

    def raw_to_core(j):
        return remote(mine(j), raw.at[j, a], raw_send.at[j, 1], raw_recv.at[j, 1], aa=core)

    def raw_on(j):
        return remote(raw.at[j, chip], raw.at[j, chip], raw_send.at[j, 2], raw_recv.at[j, 2], aa=core)

    def raw_start(j):
        if j < stages:
            raw_to_chip(j).start()
            raw_to_core(j).start()
            raw_local(j).start()

    def raw_forward(j):
        if j < stages:
            raw_to_chip(j).wait_recv()
            raw_on(j).start()

    def raw_finish(j):
        raw_local(j).wait()
        raw_to_core(j).wait_recv()
        raw_on(j).wait_recv()

    def permute(j):
        def step(n, _):
            at = n * e_tile
            total = jnp.zeros((3 * rows, e_tile), jnp.float32)
            for src in range(4):
                here = lax.broadcasted_iota(jnp.int32, (e_tile, columns), 0) + (a * columns + at)
                hit = here == perm_ref[src]
                onehot[src % 2] = jnp.where(hit, 1.0, 0.0).astype(jnp.bfloat16)
                total += lax.dot_general(
                    raw[j, src].reshape(3 * rows, columns), onehot[src % 2], NT_DIMS,
                    preferred_element_type=jnp.float32,
                )
            panel[j, :, pl.ds(b, 1), :, pl.ds(pl.multiple_of(at, e_tile), e_tile)] = (
                total.astype(jnp.bfloat16).reshape(3, 1, rows, e_tile)
            )
            return 0

        lax.fori_loop(0, columns // e_tile, step, 0)

    def z_copy(j, block, way, target):
        where = panel.at[j, :, block]
        return remote(where, where, z_send.at[j, way, block], z_recv.at[j, block], ba=target)

    def z_start(j):
        if j < stages:
            pl.when(has_right)(lambda: z_copy(j, b, 0, right).start())
            pl.when(has_left)(lambda: z_copy(j, b, 1, left).start())

    def hop(j, h):
        @pl.when(b - h >= 0)
        def _():
            block = jnp.maximum(b - h, 0)
            z_copy(j, block, 0, right).wait_recv()
            pl.when(has_right)(lambda: z_copy(j, block, 0, right).start())

        @pl.when(b + h < blocks)
        def _():
            block = jnp.minimum(b + h, blocks - 1)
            z_copy(j, block, 1, left).wait_recv()
            pl.when(has_left)(lambda: z_copy(j, block, 1, left).start())

    def hops(j, third):
        if j >= stages:
            return
        cuts = [1 + (blocks - 1) * i // 3 for i in range(4)]

        def step(h, _):
            hop(j, h)
            return 0

        lax.fori_loop(cuts[third], cuts[third + 1], step, 0)

    def z_done(j):
        def step(block, _):
            pl.when(jnp.logical_and(has_right, block <= b))(lambda: z_copy(j, block, 0, right).wait_send())
            pl.when(jnp.logical_and(has_left, block >= b))(lambda: z_copy(j, block, 1, left).wait_send())
            return 0

        lax.fori_loop(0, blocks, step, 0)

    def near_copies(j, hh):
        slot = j % 2
        return tuple(
            remote(
                part.at[slot, dest, :, :, lanes(hh)], near.at[slot, i, :, :, lanes(hh)],
                near_send.at[j, hh, i], near_recv.at[j, hh, i], aa=core,
            )
            for i, dest in enumerate((core, diag))
        )

    def far_copy(j, hh):
        return remote(
            part.at[j % 2, chip, :, :, lanes(hh)], far_ref.at[:, pl.ds(j * rows, rows), lanes(hh)],
            far_send.at[j, hh], far_recv.at[j, hh], aa=chip,
        )

    def own_copy(j, hh):
        return pltpu.make_async_copy(
            part.at[j % 2, a, :, :, lanes(hh)], own_ref.at[:, pl.ds(j * rows, rows), lanes(hh)], own_sem.at[j, hh]
        )

    def leave(j, hh):
        for copy in near_copies(j, hh):
            copy.wait_send()
        far_copy(j, hh).wait_send()
        own_copy(j, hh).wait()

    def product(j, hh):
        slot = j % 2
        if j >= 2:
            leave(j - 2, hh)

        def step(t, _):
            count = j * tiles + t
            now = count % 2

            @pl.when(count + 1 < stages * tiles)
            def _():
                for copy in w_copies((t + 1) % tiles, 1 - now):
                    copy.start()

            for copy in w_copies(t, now):
                copy.wait()
            lhs = [panel[j, kind].reshape(blocks * rows, columns) for kind in range(3)]
            total = lax.dot_general(lhs[0], w_gate[now], NT_DIMS, preferred_element_type=jnp.float32)
            total += lax.dot_general(lhs[1], w_up[now], NT_DIMS, preferred_element_type=jnp.float32)
            total += jnp.dot(lhs[2], w_down[now], preferred_element_type=jnp.float32)
            part[slot, :, :, :, pl.ds(pl.multiple_of(t * tile, tile), tile)] = total.reshape(4, group, rows, tile)
            return 0

        lax.fori_loop(*halves[hh], step, 0)
        if j >= 2:
            pl.semaphore_wait(credit.at[j - 2, hh], 1)
        for copy in near_copies(j, hh):
            copy.start()

    def combine(j, hh):
        slot = j % 2
        for copy in near_copies(j, hh):
            copy.wait_recv()

        def step(t, _):
            where = pl.ds(pl.multiple_of(t * tile, tile), tile)
            for i, dest in ((1, chip), (0, a)):
                part[slot, dest, :, :, where] = part[slot, dest, :, :, where] + near[slot, i, :, :, where]
            return 0

        lax.fori_loop(*halves[hh], step, 0)
        far_copy(j, hh).start()
        own_copy(j, hh).start()
        if j + 2 < stages:
            pl.semaphore_signal(credit.at[j, hh], inc=1, device_id={"aa": core}, device_id_type=MESH)

    for copy in w_copies(0, 0):
        copy.start()
    barrier = pltpu.get_barrier_semaphore()
    pl.semaphore_signal(barrier, inc=1, device_id={"aa": core}, device_id_type=MESH)
    pl.semaphore_signal(barrier, inc=1, device_id={"aa": chip}, device_id_type=MESH)
    pl.when(has_left)(
        lambda: pl.semaphore_signal(barrier, inc=1, device_id={"ba": left}, device_id_type=MESH)
    )
    pl.when(has_right)(
        lambda: pl.semaphore_signal(barrier, inc=1, device_id={"ba": right}, device_id_type=MESH)
    )
    pl.semaphore_wait(barrier, 2 + has_left.astype(jnp.int32) + has_right.astype(jnp.int32))

    raw_start(0)
    raw_start(1)
    raw_forward(0)
    raw_finish(0)
    raw_start(2)
    permute(0)
    z_start(0)
    raw_forward(1)
    for j in range(stages + 1):
        if j + 1 < stages:
            raw_finish(j + 1)
            raw_start(j + 3)
            permute(j + 1)
            raw_forward(j + 2)
        if j >= 2:
            combine(j - 2, 1)
        hops(j, 0)
        if j >= 1:
            product(j - 1, 0)
        hops(j, 1)
        z_start(j + 1)
        if j >= 1:
            product(j - 1, 1)
            combine(j - 1, 0)
        hops(j, 2)
    combine(stages - 1, 1)
    for j in range(max(stages - 2, 0), stages):
        leave(j, 0)
        leave(j, 1)
    for j in range(stages):
        raw_to_chip(j).wait_send()
        raw_to_core(j).wait_send()
        raw_on(j).wait_send()
        z_done(j)
        far_copy(j, 0).wait_recv()
        far_copy(j, 1).wait_recv()


def shards(mesh, gate_first, up_first, down_first, gate_second, up_second, down_second, perm):
    blocks = mesh.shape["ba"]
    assert mesh.shape["aa"] == 4 and blocks % 4 == 0
    rows_dev, columns = gate_first.shape
    units = gate_second.shape[0]
    stages = max(1, min(4, rows_dev // 16))
    rows = rows_dev // stages
    group = blocks // 4
    tile = next(t for t in (256, 128) if units % t == 0)
    e_tile = 256
    first = jnp.stack([gate_first, up_first, jnp.transpose(down_first)])
    order = perm.reshape(4, 1, columns)
    bf16, f32, dma = jnp.bfloat16, jnp.float32, pltpu.SemaphoreType.DMA
    anywhere = pl.BlockSpec(memory_space=pl.ANY)
    sums = jax.ShapeDtypeStruct((group, rows_dev, units), f32)
    own, far = pl.pallas_call(
        functools.partial(kernel, stages, blocks, rows, tile, e_tile),
        out_shape=[sums, sums],
        in_specs=[anywhere, pl.BlockSpec(memory_space=pltpu.VMEM), anywhere, anywhere, anywhere],
        out_specs=[anywhere, anywhere],
        scratch_shapes=[
            pltpu.VMEM((stages, 4, 3, rows, columns), bf16),
            pltpu.VMEM((stages, 3, blocks, rows, columns), bf16),
            pltpu.VMEM((2, 4, group, rows, units), f32),
            pltpu.VMEM((2, 2, group, rows, units), f32),
            pltpu.VMEM((2, tile, columns), bf16),
            pltpu.VMEM((2, tile, columns), bf16),
            pltpu.VMEM((2, columns, tile), bf16),
            pltpu.VMEM((2, e_tile, columns), bf16),
            dma((2, 3)),
            dma((stages,)),
            dma((stages, 3)),
            dma((stages, 3)),
            dma((stages, blocks)),
            dma((stages, 2, blocks)),
            dma((stages, 2, 2)),
            dma((stages, 2, 2)),
            dma((stages, 2)),
            dma((stages, 2)),
            dma((stages, 2)),
            pltpu.SemaphoreType.REGULAR((stages, 2)),
        ],
        compiler_params=pltpu.CompilerParams(
            collective_id=0, has_side_effects=True, vmem_limit_bytes=60 * 1024 * 1024
        ),
        cost_estimate=pl.CostEstimate(
            flops=6 * blocks * rows_dev * units * columns, bytes_accessed=6 * units * columns * stages, transcendentals=0
        ),
    )(first, order, gate_second, up_second, down_second)
    return (own + far).reshape(group * rows_dev, units)


def solution(mesh):
    placed = (
        P(("grp", "ba"), "aa"),
        P(("grp", "ba"), "aa"),
        P("aa", ("grp", "ba")),
        P(("grp", "ba"), "aa"),
        P(("grp", "ba"), "aa"),
        P("aa", ("grp", "ba")),
        P("grp"),
    )
    return jax.shard_map(
        functools.partial(shards, mesh), mesh=mesh, in_specs=placed, out_specs=P(("grp", "aa"), "ba"), check_vma=False
    )
```

```python
import functools

import jax
import jax.numpy as jnp
from jax import lax
from jax.experimental import pallas as pl
from jax.experimental.pallas import tpu as pltpu
from jax.sharding import PartitionSpec as P

MESH = pl.DeviceIdType.MESH
NT_DIMS = (((1,), (1,)), ((), ()))


def kernel(
    stages, blocks, rows, tile, e_tile,
    first_ref, perm_ref, gate_ref, up_ref, down_ref,
    own_ref, far_ref,
    raw, panel, part, near, w_gate, w_up, w_down, onehot,
    w_sem, raw_here, raw_recv, raw_send, z_recv, z_send, near_recv, near_send, far_recv, far_send, own_sem, credit,
):
    columns = first_ref.shape[2]
    units = gate_ref.shape[0]
    half = units // 2
    group = blocks // 4
    a = lax.axis_index("aa")
    b = lax.axis_index("ba")
    core = a + 1 - 2 * (a % 2)
    chip = (a + 2) % 4
    diag = (core + 2) % 4
    has_left, has_right = b > 0, b < blocks - 1
    left, right = jnp.maximum(b - 1, 0), jnp.minimum(b + 1, blocks - 1)

    tiles = units // tile
    split = (tiles + 1) // 2
    halves = ((0, split), (split, tiles))

    def lanes(hh):
        return pl.ds(halves[hh][0] * tile, (halves[hh][1] - halves[hh][0]) * tile)

    def w_copies(t, slot):
        where = pl.ds(t * tile, tile)
        return (
            pltpu.make_async_copy(gate_ref.at[where, :], w_gate.at[slot], w_sem.at[slot, 0]),
            pltpu.make_async_copy(up_ref.at[where, :], w_up.at[slot], w_sem.at[slot, 1]),
            pltpu.make_async_copy(down_ref.at[:, where], w_down.at[slot], w_sem.at[slot, 2]),
        )

    def remote(src, dst, send, recv, **to):
        return pltpu.make_async_remote_copy(
            src_ref=src, dst_ref=dst, send_sem=send, recv_sem=recv, device_id=to, device_id_type=MESH
        )

    def mine(j):
        return first_ref.at[:, pl.ds(j * rows, rows), :]

    def raw_local(j):
        return pltpu.make_async_copy(mine(j), raw.at[a, j], raw_here.at[j])

    def raw_to_chip(j):
        return remote(mine(j), raw.at[a, j], raw_send.at[j, 0], raw_recv.at[j, 0], aa=chip)

    def raw_to_core(j):
        return remote(mine(j), raw.at[a, j], raw_send.at[j, 1], raw_recv.at[j, 1], aa=core)

    def raw_on(j):
        return remote(raw.at[chip, j], raw.at[chip, j], raw_send.at[j, 2], raw_recv.at[j, 2], aa=core)

    def raw_start(j):
        if j < stages:
            raw_to_chip(j).start()
            raw_to_core(j).start()
            raw_local(j).start()

    def raw_forward(j):
        if j < stages:
            raw_to_chip(j).wait_recv()
            raw_on(j).start()

    def raw_finish(j):
        raw_local(j).wait()
        raw_to_core(j).wait_recv()
        raw_on(j).wait_recv()

    def permute(j, count=1):
        def step(n, _):
            at = n * e_tile
            total = jnp.zeros((count * 3 * rows, e_tile), jnp.float32)
            here = lax.broadcasted_iota(jnp.int32, (e_tile, columns), 0)
            for src in range(4):
                hit = here == perm_ref[src] - (a * columns + at)
                onehot[src % 2] = jnp.where(hit, 1.0, 0.0).astype(jnp.bfloat16)
                total += lax.dot_general(
                    raw[src, j : j + count].reshape(count * 3 * rows, columns), onehot[src % 2], NT_DIMS,
                    preferred_element_type=jnp.float32,
                )
            panel[j : j + count, :, pl.ds(b, 1), :, pl.ds(pl.multiple_of(at, e_tile), e_tile)] = (
                total.astype(jnp.bfloat16).reshape(count, 3, 1, rows, e_tile)
            )
            return 0

        lax.fori_loop(0, columns // e_tile, step, 0)

    def z_copy(j, block, way, target):
        where = panel.at[j, :, block]
        return remote(where, where, z_send.at[j, way, block], z_recv.at[j, block], ba=target)

    def z_start(j):
        if j < stages:
            pl.when(has_right)(lambda: z_copy(j, b, 0, right).start())
            pl.when(has_left)(lambda: z_copy(j, b, 1, left).start())

    def hop(j, h):
        @pl.when(b - h >= 0)
        def _():
            block = jnp.maximum(b - h, 0)
            z_copy(j, block, 0, right).wait_recv()
            pl.when(has_right)(lambda: z_copy(j, block, 0, right).start())

        @pl.when(b + h < blocks)
        def _():
            block = jnp.minimum(b + h, blocks - 1)
            z_copy(j, block, 1, left).wait_recv()
            pl.when(has_left)(lambda: z_copy(j, block, 1, left).start())

    def hops(j, third):
        if j >= stages:
            return
        cuts = [1 + (blocks - 1) * i // 3 for i in range(4)]

        def step(h, _):
            hop(j, h)
            return 0

        lax.fori_loop(cuts[third], cuts[third + 1], step, 0)

    def z_done(j):
        def step(block, _):
            pl.when(jnp.logical_and(has_right, block <= b))(lambda: z_copy(j, block, 0, right).wait_send())
            pl.when(jnp.logical_and(has_left, block >= b))(lambda: z_copy(j, block, 1, left).wait_send())
            return 0

        lax.fori_loop(0, blocks, step, 0)

    def near_copies(j, hh):
        slot = j % 2
        return tuple(
            remote(
                part.at[slot, dest, :, :, lanes(hh)], near.at[slot, i, :, :, lanes(hh)],
                near_send.at[j, hh, i], near_recv.at[j, hh, i], aa=core,
            )
            for i, dest in enumerate((core, diag))
        )

    def far_copy(j, hh):
        return remote(
            part.at[j % 2, chip, :, :, lanes(hh)], far_ref.at[:, pl.ds(j * rows, rows), lanes(hh)],
            far_send.at[j, hh], far_recv.at[j, hh], aa=chip,
        )

    def own_copy(j, hh):
        return pltpu.make_async_copy(
            part.at[j % 2, a, :, :, lanes(hh)], own_ref.at[:, pl.ds(j * rows, rows), lanes(hh)], own_sem.at[j, hh]
        )

    def leave(j, hh):
        for copy in near_copies(j, hh):
            copy.wait_send()
        far_copy(j, hh).wait_send()
        own_copy(j, hh).wait()

    def product(j, hh):
        slot = j % 2
        if j >= 2:
            leave(j - 2, hh)

        def step(t, _):
            count = j * tiles + t
            now = count % 2

            @pl.when(count + 1 < stages * tiles)
            def _():
                for copy in w_copies((t + 1) % tiles, 1 - now):
                    copy.start()

            for copy in w_copies(t, now):
                copy.wait()
            lhs = [panel[j, kind].reshape(blocks * rows, columns) for kind in range(3)]
            total = lax.dot_general(lhs[0], w_gate[now], NT_DIMS, preferred_element_type=jnp.float32)
            total += lax.dot_general(lhs[1], w_up[now], NT_DIMS, preferred_element_type=jnp.float32)
            total += jnp.dot(lhs[2], w_down[now], preferred_element_type=jnp.float32)
            part[slot, :, :, :, pl.ds(pl.multiple_of(t * tile, tile), tile)] = total.reshape(4, group, rows, tile)
            return 0

        lax.fori_loop(*halves[hh], step, 0)
        if j >= 2:
            pl.semaphore_wait(credit.at[j - 2, hh], 1)
        for copy in near_copies(j, hh):
            copy.start()

    def combine(j, hh):
        slot = j % 2
        for copy in near_copies(j, hh):
            copy.wait_recv()

        def step(t, _):
            where = pl.ds(pl.multiple_of(t * tile, tile), tile)
            for i, dest in ((1, chip), (0, a)):
                part[slot, dest, :, :, where] = part[slot, dest, :, :, where] + near[slot, i, :, :, where]
            return 0

        lax.fori_loop(*halves[hh], step, 0)
        far_copy(j, hh).start()
        own_copy(j, hh).start()
        if j + 2 < stages:
            pl.semaphore_signal(credit.at[j, hh], inc=1, device_id={"aa": core}, device_id_type=MESH)

    for copy in w_copies(0, 0):
        copy.start()
    barrier = pltpu.get_barrier_semaphore()
    pl.semaphore_signal(barrier, inc=1, device_id={"aa": core}, device_id_type=MESH)
    pl.semaphore_signal(barrier, inc=1, device_id={"aa": chip}, device_id_type=MESH)
    pl.when(has_left)(
        lambda: pl.semaphore_signal(barrier, inc=1, device_id={"ba": left}, device_id_type=MESH)
    )
    pl.when(has_right)(
        lambda: pl.semaphore_signal(barrier, inc=1, device_id={"ba": right}, device_id_type=MESH)
    )
    pl.semaphore_wait(barrier, 2 + has_left.astype(jnp.int32) + has_right.astype(jnp.int32))

    raw_start(0)
    raw_start(1)
    raw_forward(0)
    raw_finish(0)
    raw_start(2)
    permute(0)
    z_start(0)
    raw_forward(1)
    for j in range(stages + 1):
        if j == 0 and stages > 1:
            raw_finish(1)
            for later in range(3, stages):
                raw_start(later)
            permute(1)
            raw_forward(2)
        if j >= 2:
            combine(j - 2, 1)
        hops(j, 0)
        if j >= 1:
            product(j - 1, 0)
        hops(j, 1)
        z_start(j + 1)
        if j == 0 and stages > 2:
            for later in range(2, stages):
                if later > 2:
                    raw_forward(later)
                raw_finish(later)
            permute(2, stages - 2)
        if j >= 1:
            product(j - 1, 1)
            combine(j - 1, 0)
        hops(j, 2)
    combine(stages - 1, 1)
    for j in range(max(stages - 2, 0), stages):
        leave(j, 0)
        leave(j, 1)
    for j in range(stages):
        raw_to_chip(j).wait_send()
        raw_to_core(j).wait_send()
        raw_on(j).wait_send()
        z_done(j)
        far_copy(j, 0).wait_recv()
        far_copy(j, 1).wait_recv()


def shards(mesh, gate_first, up_first, down_first, gate_second, up_second, down_second, perm):
    blocks = mesh.shape["ba"]
    assert mesh.shape["aa"] == 4 and blocks % 4 == 0
    rows_dev, columns = gate_first.shape
    units = gate_second.shape[0]
    stages = max(1, min(4, rows_dev // 16))
    rows = rows_dev // stages
    group = blocks // 4
    tile = next(t for t in (256, 128) if units % t == 0)
    e_tile = 256
    first = jnp.stack([gate_first, up_first, jnp.transpose(down_first)])
    order = perm.reshape(4, 1, columns)
    bf16, f32, dma = jnp.bfloat16, jnp.float32, pltpu.SemaphoreType.DMA
    anywhere = pl.BlockSpec(memory_space=pl.ANY)
    sums = jax.ShapeDtypeStruct((group, rows_dev, units), f32)
    own, far = pl.pallas_call(
        functools.partial(kernel, stages, blocks, rows, tile, e_tile),
        out_shape=[sums, sums],
        in_specs=[anywhere, pl.BlockSpec(memory_space=pltpu.VMEM), anywhere, anywhere, anywhere],
        out_specs=[anywhere, anywhere],
        scratch_shapes=[
            pltpu.VMEM((4, stages, 3, rows, columns), bf16),
            pltpu.VMEM((stages, 3, blocks, rows, columns), bf16),
            pltpu.VMEM((2, 4, group, rows, units), f32),
            pltpu.VMEM((2, 2, group, rows, units), f32),
            pltpu.VMEM((2, tile, columns), bf16),
            pltpu.VMEM((2, tile, columns), bf16),
            pltpu.VMEM((2, columns, tile), bf16),
            pltpu.VMEM((2, e_tile, columns), bf16),
            dma((2, 3)),
            dma((stages,)),
            dma((stages, 3)),
            dma((stages, 3)),
            dma((stages, blocks)),
            dma((stages, 2, blocks)),
            dma((stages, 2, 2)),
            dma((stages, 2, 2)),
            dma((stages, 2)),
            dma((stages, 2)),
            dma((stages, 2)),
            pltpu.SemaphoreType.REGULAR((stages, 2)),
        ],
        compiler_params=pltpu.CompilerParams(
            collective_id=0, has_side_effects=True, vmem_limit_bytes=60 * 1024 * 1024
        ),
        cost_estimate=pl.CostEstimate(
            flops=6 * blocks * rows_dev * units * columns, bytes_accessed=6 * units * columns * stages, transcendentals=0
        ),
    )(first, order, gate_second, up_second, down_second)
    return (own + far).reshape(group * rows_dev, units)


def solution(mesh):
    placed = (
        P(("grp", "ba"), "aa"),
        P(("grp", "ba"), "aa"),
        P("aa", ("grp", "ba")),
        P(("grp", "ba"), "aa"),
        P(("grp", "ba"), "aa"),
        P("aa", ("grp", "ba")),
        P("grp"),
    )
    return jax.shard_map(
        functools.partial(shards, mesh), mesh=mesh, in_specs=placed, out_specs=P(("grp", "aa"), "ba"), check_vma=False
    )
```
